32 devices in a mesh: band: 4 (over y, x), col: 8 (over z, core).
Axes of the slice: x: 2, y: 2, z: 4, core: 2. Of those that a mesh axis runs over, the one named last changes fastest.
Arguments:
- obs_priors: float32 [80, 16384], P(None, ('band', 'col')), may hold values from -0.375 to 0.375
- innovation: float32 [16384], P(('band', 'col')), may hold values from -6 to 6
- obs_precision: float32 [16384], P(('band', 'col')), may hold values from 0.25 to 4
- tile_block: int32 [128], P(('band', 'col')), may hold values from 0 to 3
- obs_count: int32 [32], P(('band', 'col')), may hold values from 128 to 512
- block_mask: int32 [4, 32], P(None, 'col'), may hold values 0 or 1
- prior_state_mean: float32 [32, 16, 1024], P('col', None, 'band'), may hold values from -6 to 6
- prior_state_deviation: float32 [32, 16, 80, 1024], P('col', None, None, 'band'), may hold values from -6 to 6
Outputs:
- posterior_mean: float32 [32, 16, 1024], P('col', None, 'band')
- analysis_perturb: float32 [32, 16, 80, 1024], P('col', None, None, 'band')
The draws below stay inside these ranges and needn't reach their ends.
All inputs are finite; a program needn't handle non-finite values. No bound on the sum of `block_mask` on one device may be relied on, other than what follows from the above.
Results may differ from the reference program's by a relative error of at most 0.0001.
Values sent between devices are 32-bit elements; how exact they have to be, the bound alone decides.
A program may use at most 64 MiB of HBM per device.

```python
import math
import jax
import jax.numpy as jnp
from jax import lax

K = 80
G_DEV = 4
LEV = 16
TILE = 128
TILES_DEV = 4
OBS_DEV = 512
NBANDS = 4
BLOCKS = 32
COLS = 1024
NOBS = 16384
NTILES = 128
GROUP_COUNT = 32
N_COL = 8


def with_ends(result, key, smallest, top_value):
    place = [jax.random.randint(jax.random.fold_in(key, axis), (), 0, length) for axis, length in enumerate(result.shape)]
    main_axis = result.shape.index(max(result.shape))
    beside = place[:main_axis] + [(place[main_axis] + 1) % result.shape[main_axis]] + place[main_axis + 1:]
    return result.at[tuple(place)].set(smallest).at[tuple(beside)].set(top_value)


def block_levels(own_key, dims, pieces, least, top_value):
    level = 1.0
    for axis_at, shards_of in pieces:
        steps = jax.random.uniform(jax.random.fold_in(jax.random.fold_in(own_key, 6), axis_at), (shards_of,), jnp.float32, least / len(pieces), top_value / len(pieces))
        level = level * jnp.repeat(jnp.exp(steps), dims[axis_at] // shards_of).reshape((-1,) + (1,) * (len(dims) - 1 - axis_at))
    return level


def centred(own_key, extent, scale, reach, pieces=(), held_as=jnp.bfloat16):
    drawn = jax.random.normal(own_key, extent, jnp.float32) * scale
    if len(pieces) > 0:
        drawn = block_levels(own_key, extent, pieces, -0.22, 0.18) * drawn
    return jnp.clip(drawn, min=-reach, max=reach).astype(held_as)


def setup_inputs(seed: int = 0) -> dict:
    keys = jax.random.split(jax.random.key(seed), 9)
    obs_priors = centred(keys[0], (K, NOBS), (4.0 * (N_COL * OBS_DEV) ** -0.5), 0.375, ((1, 32),), jnp.float32)
    innovation = centred(keys[1], (NOBS,), 1.0, 6.0, ((0, 32),), jnp.float32)
    obs_precision = jnp.clip(jnp.exp(math.log(4.0) - 2.7725887 * jax.random.uniform(keys[2], (NOBS,), jnp.float32) ** block_levels(keys[2], (NOBS,), ((0, 32),), -0.2, 0.2)), 0.25, 4.0)
    tile_block = with_ends(jax.random.randint(keys[3], (NTILES,), 0, G_DEV), jax.random.fold_in(keys[3], 1), 0, G_DEV - 1).astype(jnp.int32)
    obs_count = with_ends(jax.random.randint(keys[4], (GROUP_COUNT,), TILE, OBS_DEV + 1), jax.random.fold_in(keys[4], 1), TILE, OBS_DEV).astype(jnp.int32)
    block_mask = with_ends((jax.random.randint(keys[5], (NBANDS, BLOCKS), 0, 4) < 3).astype(jnp.int32), jax.random.fold_in(keys[5], 1), 0, 1)
    prior_state_mean = centred(keys[6], (BLOCKS, LEV, COLS), 1.0, 6.0, ((0, 8), (2, 4)), jnp.float32)
    prior_state_deviation = centred(keys[7], (BLOCKS, LEV, K, COLS), 1.0, 6.0, ((0, 8), (3, 4)), jnp.float32)
    return {"obs_priors": obs_priors, "innovation": innovation, "obs_precision": obs_precision, "tile_block": tile_block, "obs_count": obs_count, "block_mask": block_mask, "prior_state_mean": prior_state_mean, "prior_state_deviation": prior_state_deviation}


PRECISION_HIGH = lax.Precision.HIGHEST

def reference(obs_priors, innovation, obs_precision, tile_block, obs_count, block_mask, prior_state_mean, prior_state_deviation):
    ensemble_members = obs_priors.shape[0]
    group_rows = N_COL * OBS_DEV
    identity = jnp.eye(ensemble_members, dtype=jnp.float32)
    affine_update = jnp.concatenate([jnp.broadcast_to(identity, (BLOCKS, ensemble_members, ensemble_members)), jnp.zeros((BLOCKS, ensemble_members, 1), jnp.float32)], axis=2)
    row_index = jnp.arange(OBS_DEV, dtype=jnp.int32)
    col_base = (jnp.arange(N_COL, dtype=jnp.int32) * G_DEV)[:, None]
    for band_index in range(NBANDS):
        priors = obs_priors[:, band_index * group_rows:(band_index + 1) * group_rows].reshape(ensemble_members, N_COL * TILES_DEV, TILE)
        innov_tiles = innovation[band_index * group_rows:(band_index + 1) * group_rows].reshape(N_COL * TILES_DEV, TILE)
        precision_tiles = obs_precision[band_index * group_rows:(band_index + 1) * group_rows]
        counts = obs_count[band_index * N_COL:(band_index + 1) * N_COL]
        live_rows = (row_index[None, :] < counts[:, None]).reshape(N_COL * TILES_DEV, TILE)
        weights = jnp.where(live_rows, precision_tiles.reshape(N_COL * TILES_DEV, TILE), jnp.float32(0.0))
        blocks_here = tile_block[band_index * N_COL * TILES_DEV:(band_index + 1) * N_COL * TILES_DEV].reshape(N_COL, TILES_DEV)
        global_block = (col_base + blocks_here).reshape(-1).astype(jnp.int32)
        tile_maps = affine_update[global_block]
        updated = jnp.einsum('tkl,ktr->ltr', tile_maps, priors, precision=PRECISION_HIGH)
        spread = updated[:ensemble_members]
        departure = innov_tiles - updated[ensemble_members]
        curvature = jnp.einsum('ltr,tr,mtr->lm', spread, weights, spread, precision=PRECISION_HIGH)
        projected = jnp.einsum('ltr,tr->l', spread, weights * departure, precision=PRECISION_HIGH)
        system = (ensemble_members - 1) * identity + curvature
        factor = jnp.linalg.cholesky(system)
        solved = jax.scipy.linalg.cho_solve((factor, True), jnp.concatenate([projected[:, None], curvature], axis=1))
        ensemble_transform = identity - 0.5 * solved[:, 1:]
        augmented = jnp.zeros((ensemble_members + 1, ensemble_members + 1), jnp.float32)
        augmented = augmented.at[:ensemble_members, :ensemble_members].set(ensemble_transform)
        augmented = augmented.at[:ensemble_members, ensemble_members].set(solved[:, 0])
        augmented = augmented.at[ensemble_members, ensemble_members].set(1.0)
        moved = jnp.einsum('gkl,lm->gkm', affine_update, augmented, precision=PRECISION_HIGH)
        apply_flags = block_mask[band_index] > 0
        affine_update = jnp.where(apply_flags[:, None, None], moved, affine_update)
    posterior_mean = prior_state_mean + jnp.einsum('eu,evur->evr', affine_update[:, :, ensemble_members], prior_state_deviation, precision=PRECISION_HIGH)
    analysis_perturb = jnp.einsum('gkm,glkc->glmc', affine_update[:, :, :ensemble_members], prior_state_deviation, precision=PRECISION_HIGH)
    return (posterior_mean, analysis_perturb)
```

```python
import functools

import jax
import jax.numpy as jnp
from jax import lax
from jax.experimental import pallas as pl
from jax.experimental.pallas import tpu as pltpu
from jax.sharding import PartitionSpec as P

HIGHEST = lax.Precision.HIGHEST
F32 = jnp.float32
BF16 = jnp.bfloat16
ROWS = 8
LANES = 128


def iota(shape, axis):
    return lax.broadcasted_iota(jnp.int32, shape, axis)


def spread_row(x, k):
    return jnp.broadcast_to(x[k : k + 1, :], x.shape)


def spread_lane(x, k):
    return jnp.broadcast_to(x[:, k : k + 1], x.shape)


def dot(a, b):
    return lax.dot_general(
        a, b, (((1,), (0,)), ((), ())), precision=HIGHEST, preferred_element_type=F32
    )


def invert(system, members):
    count = members // ROWS
    parts = [system[i * ROWS : (i + 1) * ROWS] for i in range(count)]
    row = iota((ROWS, LANES), 0)
    lane = iota((ROWS, LANES), 1)
    for j in range(count):
        base = j * ROWS
        cols = [[spread_lane(parts[i], base + c) for c in range(ROWS)] for i in range(count)]
        inside = (lane >= base) & (lane < base + ROWS)
        unit = jnp.where(lane - base == row, F32(1.0), F32(0.0))
        panel = jnp.where(inside, unit, parts[j])
        own = list(cols[j])
        for k in range(ROWS):
            inverse = 1.0 / spread_row(own[k], k)
            factor = jnp.where(row == k, own[k] - 1.0, own[k]) * inverse
            for c in range(k + 1, ROWS):
                own[c] = own[c] - factor * spread_row(own[c], k)
            panel = panel - factor * spread_row(panel, k)
        spread = [spread_row(panel, c) for c in range(ROWS)]
        for i in range(count):
            if i == j:
                continue
            terms = [cols[i][c] * spread[c] for c in range(ROWS)]
            while len(terms) > 1:
                terms = [a + b for a, b in zip(terms[::2], terms[1::2])]
            parts[i] = jnp.where(inside, F32(0.0), parts[i]) - terms[0]
        parts[j] = panel
    return jnp.concatenate(parts, axis=0)


def chain(grams, flags, members, bands, blocks):
    lane = iota((members, LANES), 1)
    diagonal = lane == iota((members, LANES), 0)
    start = jnp.where(diagonal, F32(1.0), F32(0.0))
    maps = [start] * blocks
    tail_lane = iota((LANES - members, LANES), 1)
    tail_row = iota((LANES - members, LANES), 0)
    tail = jnp.where((tail_row == 0) & (tail_lane == members), F32(1.0), F32(0.0))
    for b in range(bands):
        system = grams[b][0] + jnp.where(diagonal, F32(members - 1), F32(0.0))
        solved = invert(system, members)
        half = jnp.where(diagonal, F32(0.5), F32(0.0)) + (0.5 * (members - 1)) * solved
        top = jnp.where(lane == members, -solved, half)
        step = jnp.concatenate([top, tail], axis=0)
        square = jnp.where(lane < members, top, F32(0.0))
        square = jnp.concatenate([square, jnp.zeros_like(tail)], axis=0)
        for later in range(b + 1, bands):
            old = grams[later]
            count = len(old) // 2
            new = []
            for r in range(count):
                right = dot(old[2 * r + 1], step)
                right = jnp.concatenate([right, jnp.zeros_like(tail)], axis=0)
                new.append(old[2 * r] + dot(square[:members], right))
            grams[later] = new
        moved = dot(jnp.concatenate(maps, axis=0), step)
        for g in range(blocks):
            here = moved[g * members : (g + 1) * members]
            maps[g] = jnp.where(flags[b][g] > 0, here, maps[g])
    return maps


def apply_maps(maps, mean_ref, high_ref, low_ref, out_ref, out_hbm, out_sems, left_ref, mean_out):
    blocks, levels, members, columns = out_ref.shape
    halves = out_sems.shape[1]
    step = levels // halves
    for g in range(blocks):
        high = maps[g].astype(BF16).astype(F32)
        low = maps[g] - high
        pad = jnp.zeros((2 * LANES - 3 * members, LANES), F32)
        stacked = jnp.concatenate([high, low, high, pad], axis=0)
        left = jnp.concatenate([stacked[:LANES].T, stacked[LANES:].T], axis=1)
        left_ref[g] = left[: members + ROWS].astype(BF16)

    def block(g, carry):
        left = left_ref[g][:, : 3 * members]
        for h in range(halves):
            for l in range(h * step, (h + 1) * step):
                high = high_ref[g, l]
                right = jnp.concatenate([high, high, low_ref[g, l]], axis=0)
                result = jnp.dot(left, right, preferred_element_type=F32)
                out_ref[g, l] = result[:members]
                mean_out[g, l : l + 1, :] = mean_ref[g, l : l + 1, :] - result[members : members + 1]
            here = pl.ds(h * step, step)
            pltpu.make_async_copy(
                out_ref.at[g, here], out_hbm.at[g, here], out_sems.at[g, h]
            ).start()
        return carry

    lax.fori_loop(0, blocks, block, 0)
    for g in range(blocks):
        for h in range(halves):
            here = pl.ds(h * step, step)
            pltpu.make_async_copy(
                out_ref.at[g, here], out_hbm.at[g, here], out_sems.at[g, h]
            ).wait()


def kernel(
    bands, flag_ref, gram_ref, mean_ref, state_hbm, mean_out, out_hbm,
    state_ref, high_ref, low_ref, out_ref, left_ref, in_sems, out_sems,
):
    blocks, levels, members, columns = state_hbm.shape
    for g in range(blocks):
        pltpu.make_async_copy(state_hbm.at[g], state_ref.at[g], in_sems.at[g]).start()
    for g in range(blocks):
        pltpu.make_async_copy(state_hbm.at[g], state_ref.at[g], in_sems.at[g]).wait()

        def split(l, carry):
            value = state_ref[g, l]
            high = value.astype(BF16)
            high_ref[g, l] = high
            low_ref[g, l] = (value - high.astype(F32)).astype(BF16)
            return carry

        lax.fori_loop(0, levels, split, 0)
    grams = []
    for b in range(bands):
        first = 2**b - 1
        grams.append([gram_ref[first + p] for p in range(2**b)])
    flags = [[flag_ref[b, g] for g in range(blocks)] for b in range(bands)]
    maps = chain(grams, flags, members, bands, blocks)
    apply_maps(maps, mean_ref, high_ref, low_ref, out_ref, out_hbm, out_sems, left_ref, mean_out)


def local(
    obs_priors,
    innovation,
    obs_precision,
    tile_block,
    obs_count,
    block_mask,
    prior_state_mean,
    prior_state_deviation,
):
    members, rows = obs_priors.shape
    tiles = tile_block.shape[0]
    blocks, levels, _, columns = prior_state_deviation.shape
    bands = lax.axis_size("band")
    my_band = lax.axis_index("band")
    live = jnp.arange(rows, dtype=jnp.int32) < obs_count[0]
    weights = jnp.where(live, obs_precision, F32(0.0))
    augmented = jnp.concatenate(
        [obs_priors, innovation[None], jnp.zeros((LANES - members - 1, rows), F32)], axis=0
    )
    shape = (-1, tiles, rows // tiles)
    gram = jnp.einsum(
        "ktr,ltr->tkl",
        (obs_priors * weights).reshape(shape),
        augmented.reshape(shape),
        precision=HIGHEST,
    )
    on = (block_mask > 0).astype(jnp.int32)
    band = jnp.arange(bands, dtype=jnp.int32)
    history = jnp.sum(jnp.where((band < my_band)[:, None], on << band[:, None], 0), axis=0)
    mine = tile_block[:, None] == jnp.arange(blocks, dtype=jnp.int32)[None]
    pattern = jnp.sum(jnp.where(mine, history[None], 0), axis=1)
    slot = pattern + (1 << my_band) - 1
    slots = 2**bands - 1
    chosen = (slot[:, None] == jnp.arange(slots, dtype=jnp.int32)[None]).astype(F32)
    sums = jnp.sum(chosen[:, :, None, None] * gram[:, None], axis=0)
    sums = lax.psum(sums, ("band", "col"))
    vmem = pl.BlockSpec(memory_space=pltpu.VMEM)
    hbm = pl.BlockSpec(memory_space=pl.ANY)
    halves = 2
    return pl.pallas_call(
        functools.partial(kernel, bands),
        out_shape=(
            jax.ShapeDtypeStruct(prior_state_mean.shape, F32),
            jax.ShapeDtypeStruct(prior_state_deviation.shape, F32),
        ),
        in_specs=[pl.BlockSpec(memory_space=pltpu.SMEM), vmem, vmem, hbm],
        out_specs=(vmem, hbm),
        scratch_shapes=[
            pltpu.VMEM(prior_state_deviation.shape, F32),
            pltpu.VMEM(prior_state_deviation.shape, BF16),
            pltpu.VMEM(prior_state_deviation.shape, BF16),
            pltpu.VMEM(prior_state_deviation.shape, F32),
            pltpu.VMEM((blocks, members + ROWS, 2 * LANES), BF16),
            pltpu.SemaphoreType.DMA((blocks,)),
            pltpu.SemaphoreType.DMA((blocks, halves)),
        ],
        compiler_params=pltpu.CompilerParams(vmem_limit_bytes=40 * 1024 * 1024),
    )(on, sums, prior_state_mean, prior_state_deviation)


def solution(mesh):
    placed = (
        P(None, ("band", "col")),
        P(("band", "col")),
        P(("band", "col")),
        P(("band", "col")),
        P(("band", "col")),
        P(None, "col"),
        P("col", None, "band"),
        P("col", None, None, "band"),
    )
    return jax.shard_map(
        local,
        mesh=mesh,
        in_specs=placed,
        out_specs=(P("col", None, "band"), P("col", None, None, "band")),
        check_vma=False,
    )
```

```python
import functools

import jax
import jax.numpy as jnp
from jax import lax
from jax.experimental import pallas as pl
from jax.experimental.pallas import tpu as pltpu
from jax.sharding import PartitionSpec as P

HIGHEST = lax.Precision.HIGHEST
F32 = jnp.float32
BF16 = jnp.bfloat16
ROWS = 8
LANES = 128
MESH = pl.DeviceIdType.MESH


def iota(shape, axis):
    return lax.broadcasted_iota(jnp.int32, shape, axis)


def spread_row(x, k):
    return jnp.broadcast_to(x[k : k + 1, :], x.shape)


def spread_lane(x, k):
    return jnp.broadcast_to(x[:, k : k + 1], x.shape)


def dot(a, b):
    return lax.dot_general(
        a, b, (((1,), (0,)), ((), ())), precision=HIGHEST, preferred_element_type=F32
    )


def invert(system, members):
    count = members // ROWS
    parts = [system[i * ROWS : (i + 1) * ROWS] for i in range(count)]
    row = iota((ROWS, LANES), 0)
    lane = iota((ROWS, LANES), 1)
    for j in range(count):
        base = j * ROWS
        cols = [[spread_lane(parts[i], base + c) for c in range(ROWS)] for i in range(count)]
        inside = (lane >= base) & (lane < base + ROWS)
        unit = jnp.where(lane - base == row, F32(1.0), F32(0.0))
        panel = jnp.where(inside, unit, parts[j])
        own = list(cols[j])
        for k in range(ROWS):
            inverse = 1.0 / spread_row(own[k], k)
            factor = jnp.where(row == k, own[k] - 1.0, own[k]) * inverse
            for c in range(k + 1, ROWS):
                own[c] = own[c] - factor * spread_row(own[c], k)
            panel = panel - factor * spread_row(panel, k)
        spread = [spread_row(panel, c) for c in range(ROWS)]
        for i in range(count):
            if i == j:
                continue
            terms = [cols[i][c] * spread[c] for c in range(ROWS)]
            while len(terms) > 1:
                terms = [a + b for a, b in zip(terms[::2], terms[1::2])]
            parts[i] = jnp.where(inside, F32(0.0), parts[i]) - terms[0]
        parts[j] = panel
    return jnp.concatenate(parts, axis=0)


def chain(grams, flags, members, bands, blocks):
    lane = iota((members, LANES), 1)
    diagonal = lane == iota((members, LANES), 0)
    start = jnp.where(diagonal, F32(1.0), F32(0.0))
    maps = [start] * blocks
    tail_lane = iota((LANES - members, LANES), 1)
    tail_row = iota((LANES - members, LANES), 0)
    tail = jnp.where((tail_row == 0) & (tail_lane == members), F32(1.0), F32(0.0))
    for b in range(bands):
        system = grams[b][0] + jnp.where(diagonal, F32(members - 1), F32(0.0))
        solved = invert(system, members)
        half = jnp.where(diagonal, F32(0.5), F32(0.0)) + (0.5 * (members - 1)) * solved
        top = jnp.where(lane == members, -solved, half)
        step = jnp.concatenate([top, tail], axis=0)
        square = jnp.where(lane < members, top, F32(0.0))
        square = jnp.concatenate([square, jnp.zeros_like(tail)], axis=0)
        for later in range(b + 1, bands):
            old = grams[later]
            count = len(old) // 2
            new = []
            for r in range(count):
                right = dot(old[2 * r + 1], step)
                right = jnp.concatenate([right, jnp.zeros_like(tail)], axis=0)
                new.append(old[2 * r] + dot(square[:members], right))
            grams[later] = new
        moved = dot(jnp.concatenate(maps, axis=0), step)
        for g in range(blocks):
            here = moved[g * members : (g + 1) * members]
            maps[g] = jnp.where(flags[b][g] > 0, here, maps[g])
    return maps


def apply_maps(maps, mean_ref, high_ref, low_ref, out_ref, out_hbm, out_sems, left_ref, mean_out):
    blocks, levels, members, columns = out_ref.shape
    halves = out_sems.shape[1]
    step = levels // halves
    for g in range(blocks):
        high = maps[g].astype(BF16).astype(F32)
        low = maps[g] - high
        pad = jnp.zeros((2 * LANES - 3 * members, LANES), F32)
        stacked = jnp.concatenate([high, low, high, pad], axis=0)
        left = jnp.concatenate([stacked[:LANES].T, stacked[LANES:].T], axis=1)
        left_ref[g] = left[: members + ROWS].astype(BF16)

    def block(g, carry):
        left = left_ref[g][:, : 3 * members]
        for h in range(halves):
            for l in range(h * step, (h + 1) * step):
                high = high_ref[g, l]
                right = jnp.concatenate([high, high, low_ref[g, l]], axis=0)
                result = jnp.dot(left, right, preferred_element_type=F32)
                out_ref[g, l] = result[:members]
                mean_out[g, l : l + 1, :] = mean_ref[g, l : l + 1, :] - result[members : members + 1]
            here = pl.ds(h * step, step)
            pltpu.make_async_copy(
                out_ref.at[g, here], out_hbm.at[g, here], out_sems.at[g, h]
            ).start()
        return carry

    lax.fori_loop(0, blocks, block, 0)
    for g in range(blocks):
        for h in range(halves):
            here = pl.ds(h * step, step)
            pltpu.make_async_copy(
                out_ref.at[g, here], out_hbm.at[g, here], out_sems.at[g, h]
            ).wait()


def packed_rows(members):
    rest = members - LANES // 2
    return LANES // 2, 2 * rest


def pack(total, members):
    kept, shift = packed_rows(members)
    rest = members - kept
    lane = iota((rest, LANES), 1)
    corner = pltpu.roll(total[kept:], shift, 1)
    corner = jnp.where((lane >= kept + shift) & (lane <= members + shift), corner, F32(0.0))
    return jnp.concatenate([total[:rest] + corner, total[rest:kept]], axis=0)


def unpack(packed, members):
    kept, shift = packed_rows(members)
    rest = members - kept
    lane = iota((rest, LANES), 1)
    square = jnp.concatenate([packed, jnp.zeros((LANES - kept, LANES), F32)], axis=0)
    corner = pltpu.roll(packed[:rest], LANES - shift, 1)
    lower = jnp.where(lane < kept, square.T[kept:members], corner)
    lower = jnp.where(lane <= members, lower, F32(0.0))
    upper = jnp.where(iota((kept, LANES), 1) <= members, packed, F32(0.0))
    return jnp.concatenate([upper, lower], axis=0)


def local_sums(priors_ref, innov_ref, precision_ref, tile_ref, count_ref, flag_ref, sums_ref, my_band):
    members, rows = priors_ref.shape
    tiles = tile_ref.shape[0]
    bands, blocks = flag_ref.shape
    size = rows // tiles
    live = iota((1, rows), 1) < count_ref[0]
    weighted = priors_ref[...] * jnp.where(live, precision_ref[...], F32(0.0))
    below = iota((LANES - members, rows), 0)
    below = jnp.where(below == 0, jnp.broadcast_to(innov_ref[...], below.shape), F32(0.0))
    augmented = jnp.concatenate([priors_ref[...], below], axis=0)
    history = []
    for g in range(blocks):
        bits = jnp.int32(0)
        for b in range(bands - 1):
            on = jnp.where(flag_ref[b, g] > 0, jnp.int32(2**b), jnp.int32(0))
            bits = bits + jnp.where(b < my_band, on, jnp.int32(0))
        history.append(bits)
    grams, patterns = [], []
    for t in range(tiles):
        here = slice(t * size, (t + 1) * size)
        gram = lax.dot_general(
            weighted[:, here], augmented[:, here], (((1,), (1,)), ((), ())),
            precision=HIGHEST, preferred_element_type=F32,
        )
        grams.append(pack(gram, members))
        pattern = jnp.int32(0)
        for g in range(blocks):
            pattern = pattern + jnp.where(tile_ref[t] == g, history[g], jnp.int32(0))
        patterns.append(pattern)
    for p in range(sums_ref.shape[0]):
        terms = [
            jnp.where(patterns[t] == p, F32(1.0), F32(0.0)) * grams[t] for t in range(tiles)
        ]
        sums_ref[p] = sum(terms[1:], terms[0])


def exchange_kernel(
    bands, cols, priors_ref, innov_ref, precision_ref, tile_ref, count_ref, flag_ref, final_ref,
    sums_ref, parts_ref, send_parts, recv_parts, send_all, recv_all,
):
    my_band, my_col = lax.axis_index("band"), lax.axis_index("col")
    devices = bands * cols
    me = my_band * cols + my_col
    owners = final_ref.shape[1] // ROWS
    barrier = pltpu.get_barrier_semaphore()

    def greet(d, carry):
        other = lax.rem(me + d, devices)
        pl.semaphore_signal(
            barrier, inc=1, device_id=(other // cols, lax.rem(other, cols)), device_id_type=MESH
        )
        return carry

    lax.fori_loop(1, devices, greet, 0)
    local_sums(priors_ref, innov_ref, precision_ref, tile_ref, count_ref, flag_ref, sums_ref, my_band)
    pl.semaphore_wait(barrier, devices - 1)

    def part_copy(band, source, owner):
        count = 2**band
        return pltpu.make_async_remote_copy(
            src_ref=sums_ref.at[pl.ds(0, count), pl.ds(pl.multiple_of(owner * ROWS, ROWS), ROWS)],
            dst_ref=parts_ref.at[source, pl.ds(0, count)],
            send_sem=send_parts.at[owner],
            recv_sem=recv_parts.at[source],
            device_id=(my_band, owner),
            device_id_type=MESH,
        )

    def whole_copy(band, owner, slot, other):
        here = (pl.ds(2**band - 1, 2**band), pl.ds(pl.multiple_of(owner * ROWS, ROWS), ROWS))
        return pltpu.make_async_remote_copy(
            src_ref=final_ref.at[here],
            dst_ref=final_ref.at[here],
            send_sem=send_all.at[slot],
            recv_sem=recv_all.at[band, owner],
            device_id=(other // cols, lax.rem(other, cols)),
            device_id_type=MESH,
        )

    def each_owner(action):
        def step(d, carry):
            owner = lax.rem(my_col + d, cols)

            @pl.when(owner < owners)
            def _():
                action(owner)

            return carry

        lax.fori_loop(1, cols, step, 0)

    for band in range(bands):

        @pl.when(my_band == band)
        def _(band=band):
            count = 2**band
            each_owner(lambda owner: part_copy(band, my_col, owner).start())

            @pl.when(my_col < owners)
            def _():
                rows = pl.ds(pl.multiple_of(my_col * ROWS, ROWS), ROWS)

                def add(d, total):
                    source = lax.rem(my_col + d, cols)
                    other = lax.rem(my_col + 1, cols)
                    pltpu.make_async_remote_copy(
                        src_ref=parts_ref.at[source, pl.ds(0, count)],
                        dst_ref=parts_ref.at[source, pl.ds(0, count)],
                        send_sem=send_parts.at[0],
                        recv_sem=recv_parts.at[source],
                        device_id=(my_band, other),
                        device_id_type=MESH,
                    ).wait_recv()
                    return total + parts_ref[source, :count]

                total = lax.fori_loop(1, cols, add, sums_ref[:count, rows])
                final_ref[count - 1 : 2 * count - 1, rows] = total

                def send(d, carry):
                    whole_copy(band, my_col, d - 1, lax.rem(me + d, devices)).start()
                    return carry

                lax.fori_loop(1, devices, send, 0)

    for band in range(bands):

        def receive(owner, carry, band=band):
            @pl.when((my_band != band) | (my_col != owner))
            def _():
                whole_copy(band, owner, 0, lax.rem(me + 1, devices)).wait_recv()

            return carry

        lax.fori_loop(0, owners, receive, 0)

    for band in range(bands):

        @pl.when(my_band == band)
        def _(band=band):
            each_owner(lambda owner: part_copy(band, my_col, owner).wait_send())

            @pl.when(my_col < owners)
            def _():
                def sent(d, carry):
                    whole_copy(band, my_col, d - 1, lax.rem(me + d, devices)).wait_send()
                    return carry

                lax.fori_loop(1, devices, sent, 0)


def kernel(
    bands, flag_ref, gram_ref, mean_ref, state_hbm, mean_out, out_hbm,
    state_ref, high_ref, low_ref, out_ref, left_ref, in_sems, out_sems,
):
    blocks, levels, members, columns = state_hbm.shape
    for g in range(blocks):
        pltpu.make_async_copy(state_hbm.at[g], state_ref.at[g], in_sems.at[g]).start()
    for g in range(blocks):
        pltpu.make_async_copy(state_hbm.at[g], state_ref.at[g], in_sems.at[g]).wait()

        def split(l, carry):
            value = state_ref[g, l]
            high = value.astype(BF16)
            high_ref[g, l] = high
            low_ref[g, l] = (value - high.astype(F32)).astype(BF16)
            return carry

        lax.fori_loop(0, levels, split, 0)
    grams = []
    for b in range(bands):
        first = 2**b - 1
        grams.append([unpack(gram_ref[first + p], members) for p in range(2**b)])
    flags = [[flag_ref[b, g] for g in range(blocks)] for b in range(bands)]
    maps = chain(grams, flags, members, bands, blocks)
    apply_maps(maps, mean_ref, high_ref, low_ref, out_ref, out_hbm, out_sems, left_ref, mean_out)


def local(
    obs_priors,
    innovation,
    obs_precision,
    tile_block,
    obs_count,
    block_mask,
    prior_state_mean,
    prior_state_deviation,
):
    members = obs_priors.shape[0]
    blocks, levels, _, columns = prior_state_deviation.shape
    bands = lax.axis_size("band")
    cols = lax.axis_size("col")
    kept, _ = packed_rows(members)
    owners = kept // ROWS
    smem = pl.BlockSpec(memory_space=pltpu.SMEM)
    vmem = pl.BlockSpec(memory_space=pltpu.VMEM)
    hbm = pl.BlockSpec(memory_space=pl.ANY)
    halves = 2
    sums = pl.pallas_call(
        functools.partial(exchange_kernel, bands, cols),
        out_shape=jax.ShapeDtypeStruct((2**bands - 1, kept, LANES), F32),
        in_specs=[vmem, vmem, vmem, smem, smem, smem],
        out_specs=vmem,
        scratch_shapes=[
            pltpu.VMEM((2 ** (bands - 1), kept, LANES), F32),
            pltpu.VMEM((cols, 2 ** (bands - 1), ROWS, LANES), F32),
            pltpu.SemaphoreType.DMA((owners,)),
            pltpu.SemaphoreType.DMA((cols,)),
            pltpu.SemaphoreType.DMA((bands * cols,)),
            pltpu.SemaphoreType.DMA((bands, owners)),
        ],
        compiler_params=pltpu.CompilerParams(
            collective_id=0, has_side_effects=True, vmem_limit_bytes=40 * 1024 * 1024
        ),
    )(obs_priors, innovation[None], obs_precision[None], tile_block, obs_count, block_mask)
    return pl.pallas_call(
        functools.partial(kernel, bands),
        out_shape=(
            jax.ShapeDtypeStruct(prior_state_mean.shape, F32),
            jax.ShapeDtypeStruct(prior_state_deviation.shape, F32),
        ),
        in_specs=[smem, vmem, vmem, hbm],
        out_specs=(vmem, hbm),
        scratch_shapes=[
            pltpu.VMEM(prior_state_deviation.shape, F32),
            pltpu.VMEM(prior_state_deviation.shape, BF16),
            pltpu.VMEM(prior_state_deviation.shape, BF16),
            pltpu.VMEM(prior_state_deviation.shape, F32),
            pltpu.VMEM((blocks, members + ROWS, 2 * LANES), BF16),
            pltpu.SemaphoreType.DMA((blocks,)),
            pltpu.SemaphoreType.DMA((blocks, halves)),
        ],
        compiler_params=pltpu.CompilerParams(vmem_limit_bytes=56 * 1024 * 1024),
    )(block_mask, sums, prior_state_mean, prior_state_deviation)


def solution(mesh):
    placed = (
        P(None, ("band", "col")),
        P(("band", "col")),
        P(("band", "col")),
        P(("band", "col")),
        P(("band", "col")),
        P(None, "col"),
        P("col", None, "band"),
        P("col", None, None, "band"),
    )
    return jax.shard_map(
        local,
        mesh=mesh,
        in_specs=placed,
        out_specs=(P("col", None, "band"), P("col", None, None, "band")),
        check_vma=False,
    )
```

```python
import functools

import jax
import jax.numpy as jnp
from jax import lax
from jax.experimental import pallas as pl
from jax.experimental.pallas import tpu as pltpu
from jax.sharding import PartitionSpec as P

HIGHEST = lax.Precision.HIGHEST
F32 = jnp.float32
BF16 = jnp.bfloat16
ROWS = 8
LANES = 128
MESH = pl.DeviceIdType.MESH


def iota(shape, axis):
    return lax.broadcasted_iota(jnp.int32, shape, axis)


def spread_row(x, k):
    return jnp.broadcast_to(x[k : k + 1, :], x.shape)


def spread_lane(x, k):
    return jnp.broadcast_to(x[:, k : k + 1], x.shape)


def dot(a, b):
    return lax.dot_general(
        a, b, (((1,), (0,)), ((), ())), precision=HIGHEST, preferred_element_type=F32
    )


def invert(system, members):
    count = members // ROWS
    parts = [system[i * ROWS : (i + 1) * ROWS] for i in range(count)]
    row = iota((ROWS, LANES), 0)
    lane = iota((ROWS, LANES), 1)
    for j in range(count):
        base = j * ROWS
        cols = [[spread_lane(parts[i], base + c) for c in range(ROWS)] for i in range(count)]
        inside = (lane >= base) & (lane < base + ROWS)
        unit = jnp.where(lane - base == row, F32(1.0), F32(0.0))
        panel = jnp.where(inside, unit, parts[j])
        own = list(cols[j])
        for k in range(ROWS):
            inverse = 1.0 / spread_row(own[k], k)
            factor = jnp.where(row == k, own[k] - 1.0, own[k]) * inverse
            for c in range(k + 1, ROWS):
                own[c] = own[c] - factor * spread_row(own[c], k)
            panel = panel - factor * spread_row(panel, k)
        spread = [spread_row(panel, c) for c in range(ROWS)]
        for i in range(count):
            if i == j:
                continue
            terms = [cols[i][c] * spread[c] for c in range(ROWS)]
            while len(terms) > 1:
                terms = [a + b for a, b in zip(terms[::2], terms[1::2])]
            parts[i] = jnp.where(inside, F32(0.0), parts[i]) - terms[0]
        parts[j] = panel
    return jnp.concatenate(parts, axis=0)


def packed_rows(members):
    rest = members - LANES // 2
    return LANES // 2, 2 * rest


def pack(total, members):
    kept, shift = packed_rows(members)
    rest = members - kept
    lane = iota((rest, LANES), 1)
    corner = pltpu.roll(total[kept:], shift, 1)
    corner = jnp.where((lane >= kept + shift) & (lane <= members + shift), corner, F32(0.0))
    return jnp.concatenate([total[:rest] + corner, total[rest:kept]], axis=0)


def unpack(packed, members):
    kept, shift = packed_rows(members)
    rest = members - kept
    lane = iota((rest, LANES), 1)
    square = jnp.concatenate([packed, jnp.zeros((LANES - kept, LANES), F32)], axis=0)
    corner = pltpu.roll(packed[:rest], LANES - shift, 1)
    lower = jnp.where(lane < kept, square.T[kept:members], corner)
    lower = jnp.where(lane <= members, lower, F32(0.0))
    upper = jnp.where(iota((kept, LANES), 1) <= members, packed, F32(0.0))
    return jnp.concatenate([upper, lower], axis=0)


def local_sums(priors_ref, innov_ref, precision_ref, tile_ref, count_ref, flag_ref, sums_ref, my_band):
    members, rows = priors_ref.shape
    tiles = tile_ref.shape[0]
    bands, blocks = flag_ref.shape
    size = rows // tiles
    live = iota((1, rows), 1) < count_ref[0]
    weighted = priors_ref[...] * jnp.where(live, precision_ref[...], F32(0.0))
    below = iota((LANES - members, rows), 0)
    below = jnp.where(below == 0, jnp.broadcast_to(innov_ref[...], below.shape), F32(0.0))
    augmented = jnp.concatenate([priors_ref[...], below], axis=0)
    history = []
    for g in range(blocks):
        bits = jnp.int32(0)
        for b in range(bands - 1):
            on = jnp.where(flag_ref[b, g] > 0, jnp.int32(2**b), jnp.int32(0))
            bits = bits + jnp.where(b < my_band, on, jnp.int32(0))
        history.append(bits)
    grams, patterns = [], []
    for t in range(tiles):
        here = slice(t * size, (t + 1) * size)
        gram = lax.dot_general(
            weighted[:, here], augmented[:, here], (((1,), (1,)), ((), ())),
            precision=HIGHEST, preferred_element_type=F32,
        )
        grams.append(pack(gram, members))
        pattern = jnp.int32(0)
        for g in range(blocks):
            pattern = pattern + jnp.where(tile_ref[t] == g, history[g], jnp.int32(0))
        patterns.append(pattern)
    for p in range(sums_ref.shape[0]):
        terms = [
            jnp.where(patterns[t] == p, F32(1.0), F32(0.0)) * grams[t] for t in range(tiles)
        ]
        sums_ref[p] = sum(terms[1:], terms[0])


def chain(sums_of, flag_ref, members, bands, blocks):
    lane = iota((members, LANES), 1)
    diagonal = lane == iota((members, LANES), 0)
    start = jnp.where(diagonal, F32(1.0), F32(0.0))
    maps = [start] * blocks
    tail_lane = iota((LANES - members, LANES), 1)
    tail_row = iota((LANES - members, LANES), 0)
    tail = jnp.where((tail_row == 0) & (tail_lane == members), F32(1.0), F32(0.0))
    steps = []

    def fold(sums, b):
        step, square = steps[b]
        new = []
        for r in range(len(sums) // 2):
            right = dot(sums[2 * r + 1], step)
            right = jnp.concatenate([right, jnp.zeros_like(tail)], axis=0)
            new.append(sums[2 * r] + dot(square, right))
        return new

    sums = sums_of(0)
    for b in range(bands):
        system = sums[0] + jnp.where(diagonal, F32(members - 1), F32(0.0))
        following = []
        if 0 < b < bands - 1:
            following = sums_of(b + 1)
            for k in range(b):
                following = fold(following, k)
        solved = invert(system, members)
        half = jnp.where(diagonal, F32(0.5), F32(0.0)) + (0.5 * (members - 1)) * solved
        top = jnp.where(lane == members, -solved, half)
        square = jnp.where(lane < members, top, F32(0.0))
        steps.append((jnp.concatenate([top, tail], axis=0), square))
        if b == 0 and bands > 1:
            following = sums_of(1)
        if b < bands - 1:
            sums = fold(following, b)
        moved = dot(jnp.concatenate(maps, axis=0), steps[b][0])
        for g in range(blocks):
            here = moved[g * members : (g + 1) * members]
            maps[g] = jnp.where(flag_ref[b, g] > 0, here, maps[g])
    return maps


def solve_kernel(
    bands, cols, priors_hbm, innov_hbm, precision_hbm, tile_ref, count_ref, flag_ref, left_ref,
    priors_ref, innov_ref, precision_ref, sums_ref, parts_ref, final_ref,
    in_sems, send_parts, recv_parts, send_band, recv_band, send_col, recv_col,
):
    my_band, my_col = lax.axis_index("band"), lax.axis_index("col")
    owners = final_ref.shape[1] // ROWS
    members = priors_ref.shape[0]
    blocks = flag_ref.shape[1]
    loads = [
        pltpu.make_async_copy(src, dst, in_sems.at[i])
        for i, (src, dst) in enumerate(
            [(priors_hbm, priors_ref), (innov_hbm, innov_ref), (precision_hbm, precision_ref)]
        )
    ]
    for load in loads:
        load.start()
    barrier = pltpu.get_barrier_semaphore()

    def greet_col(d, carry):
        other = lax.rem(my_col + d, cols)
        pl.semaphore_signal(barrier, inc=1, device_id=(my_band, other), device_id_type=MESH)
        return carry

    def greet_band(d, carry):
        other = lax.rem(my_band + d, bands)
        pl.semaphore_signal(barrier, inc=1, device_id=(other, my_col), device_id_type=MESH)
        return carry

    lax.fori_loop(1, cols, greet_col, 0)
    lax.fori_loop(1, bands, greet_band, 0)
    for load in loads:
        load.wait()
    local_sums(priors_ref, innov_ref, precision_ref, tile_ref, count_ref, flag_ref, sums_ref, my_band)
    pl.semaphore_wait(barrier, cols + bands - 2)

    def rows_of(owner):
        return pl.ds(pl.multiple_of(owner * ROWS, ROWS), ROWS)

    def part_copy(band, source, owner, target):
        count = 2**band
        return pltpu.make_async_remote_copy(
            src_ref=sums_ref.at[pl.ds(0, count), rows_of(owner)],
            dst_ref=parts_ref.at[source, pl.ds(0, count)],
            send_sem=send_parts.at[owner],
            recv_sem=recv_parts.at[source],
            device_id=(my_band, target),
            device_id_type=MESH,
        )

    def band_copy(band, target):
        here = (pl.ds(2**band - 1, 2**band), rows_of(my_col))
        return pltpu.make_async_remote_copy(
            src_ref=final_ref.at[here],
            dst_ref=final_ref.at[here],
            send_sem=send_band.at[target],
            recv_sem=recv_band.at[band],
            device_id=(target, my_col),
            device_id_type=MESH,
        )

    def col_copy(band, owner, target):
        here = (pl.ds(2**band - 1, 2**band), rows_of(owner))
        return pltpu.make_async_remote_copy(
            src_ref=final_ref.at[here],
            dst_ref=final_ref.at[here],
            send_sem=send_col.at[band, target],
            recv_sem=recv_col.at[band, owner],
            device_id=(my_band, target),
            device_id_type=MESH,
        )

    def each_owner(action):
        def step(d, carry):
            owner = lax.rem(my_col + d, cols)

            @pl.when(owner < owners)
            def _():
                action(owner)

            return carry

        lax.fori_loop(1, cols, step, 0)

    def each_peer(action):
        def step(d, carry):
            action(lax.rem(my_col + d, cols))
            return carry

        lax.fori_loop(1, cols, step, 0)

    def each_band(action):
        def step(d, carry):
            action(lax.rem(my_band + d, bands))
            return carry

        lax.fori_loop(1, bands, step, 0)

    for band in range(bands):

        @pl.when(my_band == band)
        def _(band=band):
            each_owner(lambda owner: part_copy(band, my_col, owner, owner).start())

    for band in range(bands):

        @pl.when((my_band == band) & (my_col < owners))
        def _(band=band):
            count = 2**band

            def add(d, total):
                source = lax.rem(my_col + d, cols)
                part_copy(band, source, my_col, source).wait_recv()
                return total + parts_ref[source, :count]

            total = lax.fori_loop(1, cols, add, sums_ref[:count, rows_of(my_col)])
            final_ref[count - 1 : 2 * count - 1, rows_of(my_col)] = total
            each_band(lambda target: band_copy(band, target).start())
            each_peer(lambda target: col_copy(band, my_col, target).start())

    def forward(band):
        @pl.when((my_band != band) & (my_col < owners))
        def _():
            band_copy(band, lax.rem(my_band + 1, bands)).wait_recv()
            each_peer(lambda target: col_copy(band, my_col, target).start())

    def sums_of(band):
        if band == 0:
            for b in range(min(bands, 3)):
                forward(b)
        elif band == 1:
            for b in range(3, bands):
                forward(b)
        each_owner(lambda owner: col_copy(band, owner, owner).wait_recv())
        first = 2**band - 1
        return [unpack(final_ref[first + p], members) for p in range(2**band)]

    maps = chain(sums_of, flag_ref, members, bands, blocks)
    for g in range(blocks):
        high = maps[g].astype(BF16).astype(F32)
        low = maps[g] - high
        pad = jnp.zeros((2 * LANES - 3 * members, LANES), F32)
        stacked = jnp.concatenate([high, low, high, pad], axis=0)
        left = jnp.concatenate([stacked[:LANES].T, stacked[LANES:].T], axis=1)
        left_ref[g] = left[: left_ref.shape[1]].astype(BF16)

    for band in range(bands):

        @pl.when(my_band == band)
        def _(band=band):
            each_owner(lambda owner: part_copy(band, my_col, owner, owner).wait_send())

            @pl.when(my_col < owners)
            def _():
                each_band(lambda target: band_copy(band, target).wait_send())

        @pl.when(my_col < owners)
        def _(band=band):
            each_peer(lambda target: col_copy(band, my_col, target).wait_send())


def apply_kernel(
    left_ref, mean_hbm, state_hbm, mean_out, out_hbm,
    state_ref, out_ref, mean_ref, moved_ref, in_sems, out_sems, mean_sems,
):
    blocks, levels, members, columns = state_hbm.shape
    pieces = in_sems.shape[0] // blocks
    size = levels // pieces

    def place(i):
        return i // pieces, pl.ds(lax.rem(i, pieces) * size, size)

    def load(i):
        here = place(i)
        return pltpu.make_async_copy(state_hbm.at[here], state_ref.at[here], in_sems.at[i])

    def store(i):
        here = place(i)
        return pltpu.make_async_copy(out_ref.at[here], out_hbm.at[here], out_sems.at[i])

    def each(action):
        def step(i, carry):
            action(i)
            return carry

        lax.fori_loop(0, blocks * pieces, step, 0)

    mean_load = pltpu.make_async_copy(mean_hbm, mean_ref, mean_sems.at[0])
    mean_load.start()
    each(lambda i: load(i).start())
    mean_load.wait()

    def work(i):
        load(i).wait()
        g = i // pieces
        left = left_ref[g][:, : 3 * members]
        for k in range(size):
            l = lax.rem(i, pieces) * size + k
            value = state_ref[g, l]
            high = value.astype(BF16)
            low = (value - high.astype(F32)).astype(BF16)
            right = jnp.concatenate([high, high, low], axis=0)
            result = jnp.dot(left, right, preferred_element_type=F32)
            out_ref[g, l] = result[:members]
            here = (g, pl.ds(l, 1))
            moved_ref[here] = mean_ref[here] - result[members : members + 1]
        store(i).start()

    each(work)
    mean_store = pltpu.make_async_copy(moved_ref, mean_out, mean_sems.at[1])
    mean_store.start()
    each(lambda i: store(i).wait())
    mean_store.wait()


def local(
    obs_priors,
    innovation,
    obs_precision,
    tile_block,
    obs_count,
    block_mask,
    prior_state_mean,
    prior_state_deviation,
):
    members, rows = obs_priors.shape
    blocks, levels, _, columns = prior_state_deviation.shape
    bands, cols = lax.axis_size("band"), lax.axis_size("col")
    kept, _ = packed_rows(members)
    owners = kept // ROWS
    smem = pl.BlockSpec(memory_space=pltpu.SMEM)
    vmem = pl.BlockSpec(memory_space=pltpu.VMEM)
    hbm = pl.BlockSpec(memory_space=pl.ANY)
    dma = pltpu.SemaphoreType.DMA
    left = pl.pallas_call(
        functools.partial(solve_kernel, bands, cols),
        out_shape=jax.ShapeDtypeStruct((blocks, members + 2 * ROWS, 2 * LANES), BF16),
        in_specs=[hbm, hbm, hbm, smem, smem, smem],
        out_specs=vmem,
        scratch_shapes=[
            pltpu.VMEM((members, rows), F32),
            pltpu.VMEM((1, rows), F32),
            pltpu.VMEM((1, rows), F32),
            pltpu.VMEM((2 ** (bands - 1), kept, LANES), F32),
            pltpu.VMEM((cols, 2 ** (bands - 1), ROWS, LANES), F32),
            pltpu.VMEM((2**bands - 1, kept, LANES), F32),
            dma((3,)),
            dma((owners,)),
            dma((cols,)),
            dma((bands,)),
            dma((bands,)),
            dma((bands, cols)),
            dma((bands, owners)),
        ],
        compiler_params=pltpu.CompilerParams(
            collective_id=0, has_side_effects=True, vmem_limit_bytes=56 * 1024 * 1024
        ),
    )(obs_priors, innovation[None], obs_precision[None], tile_block, obs_count, block_mask)
    pieces = 4
    return pl.pallas_call(
        apply_kernel,
        out_shape=(
            jax.ShapeDtypeStruct(prior_state_mean.shape, F32),
            jax.ShapeDtypeStruct(prior_state_deviation.shape, F32),
        ),
        in_specs=[vmem, hbm, hbm],
        out_specs=(hbm, hbm),
        scratch_shapes=[
            pltpu.VMEM(prior_state_deviation.shape, F32),
            pltpu.VMEM(prior_state_deviation.shape, F32),
            pltpu.VMEM(prior_state_mean.shape, F32),
            pltpu.VMEM(prior_state_mean.shape, F32),
            dma((blocks * pieces,)),
            dma((blocks * pieces,)),
            dma((2,)),
        ],
        compiler_params=pltpu.CompilerParams(vmem_limit_bytes=56 * 1024 * 1024),
    )(left, prior_state_mean, prior_state_deviation)


def solution(mesh):
    placed = (
        P(None, ("band", "col")),
        P(("band", "col")),
        P(("band", "col")),
        P(("band", "col")),
        P(("band", "col")),
        P(None, "col"),
        P("col", None, "band"),
        P("col", None, None, "band"),
    )
    return jax.shard_map(
        local,
        mesh=mesh,
        in_specs=placed,
        out_specs=(P("col", None, "band"), P("col", None, None, "band")),
        check_vma=False,
    )
```

```python
import functools

import jax
import jax.numpy as jnp
from jax import lax
from jax.experimental import pallas as pl
from jax.experimental.pallas import tpu as pltpu
from jax.sharding import PartitionSpec as P

HIGHEST = lax.Precision.HIGHEST
F32 = jnp.float32
BF16 = jnp.bfloat16
ROWS = 8
LANES = 128
MESH = pl.DeviceIdType.MESH


def iota(shape, axis):
    return lax.broadcasted_iota(jnp.int32, shape, axis)


def spread_row(x, k):
    return jnp.broadcast_to(x[k : k + 1, :], x.shape)


def spread_lane(x, k):
    return jnp.broadcast_to(x[:, k : k + 1], x.shape)


def dot(a, b):
    return lax.dot_general(
        a, b, (((1,), (0,)), ((), ())), precision=HIGHEST, preferred_element_type=F32
    )


def invert(system, members):
    count = members // ROWS
    parts = [system[i * ROWS : (i + 1) * ROWS] for i in range(count)]
    row = iota((ROWS, LANES), 0)
    lane = iota((ROWS, LANES), 1)
    for j in range(count):
        base = j * ROWS
        cols = [[spread_lane(parts[i], base + c) for c in range(ROWS)] for i in range(count)]
        inside = (lane >= base) & (lane < base + ROWS)
        unit = jnp.where(lane - base == row, F32(1.0), F32(0.0))
        panel = jnp.where(inside, unit, parts[j])
        own = list(cols[j])
        for k in range(ROWS):
            inverse = 1.0 / spread_row(own[k], k)
            factor = jnp.where(row == k, own[k] - 1.0, own[k]) * inverse
            for c in range(k + 1, ROWS):
                own[c] = own[c] - factor * spread_row(own[c], k)
            panel = panel - factor * spread_row(panel, k)
        spread = [spread_row(panel, c) for c in range(ROWS)]
        for i in range(count):
            if i == j:
                continue
            terms = [cols[i][c] * spread[c] for c in range(ROWS)]
            while len(terms) > 1:
                terms = [a + b for a, b in zip(terms[::2], terms[1::2])]
            parts[i] = jnp.where(inside, F32(0.0), parts[i]) - terms[0]
        parts[j] = panel
    return jnp.concatenate(parts, axis=0)


def packed_rows(members):
    rest = members - LANES // 2
    return LANES // 2, 2 * rest


def pack(total, members):
    kept, shift = packed_rows(members)
    rest = members - kept
    lane = iota((rest, LANES), 1)
    corner = pltpu.roll(total[kept:], shift, 1)
    corner = jnp.where((lane >= kept + shift) & (lane <= members + shift), corner, F32(0.0))
    return jnp.concatenate([total[:rest] + corner, total[rest:kept]], axis=0)


def unpack(packed, members):
    kept, shift = packed_rows(members)
    rest = members - kept
    lane = iota((rest, LANES), 1)
    square = jnp.concatenate([packed, jnp.zeros((LANES - kept, LANES), F32)], axis=0)
    corner = pltpu.roll(packed[:rest], LANES - shift, 1)
    lower = jnp.where(lane < kept, square.T[kept:members], corner)
    lower = jnp.where(lane <= members, lower, F32(0.0))
    upper = jnp.where(iota((kept, LANES), 1) <= members, packed, F32(0.0))
    return jnp.concatenate([upper, lower], axis=0)


def local_sums(priors_ref, innov_ref, precision_ref, tile_ref, count_ref, flag_ref, sums_ref, my_band):
    members, rows = priors_ref.shape
    tiles = tile_ref.shape[0]
    bands, blocks = flag_ref.shape
    size = rows // tiles
    live = iota((1, rows), 1) < count_ref[0]
    weighted = priors_ref[...] * jnp.where(live, precision_ref[...], F32(0.0))
    below = iota((LANES - members, rows), 0)
    below = jnp.where(below == 0, jnp.broadcast_to(innov_ref[...], below.shape), F32(0.0))
    augmented = jnp.concatenate([priors_ref[...], below], axis=0)
    history = []
    for g in range(blocks):
        bits = jnp.int32(0)
        for b in range(bands - 1):
            on = jnp.where(flag_ref[b, g] > 0, jnp.int32(2**b), jnp.int32(0))
            bits = bits + jnp.where(b < my_band, on, jnp.int32(0))
        history.append(bits)
    grams, patterns = [], []
    for t in range(tiles):
        here = slice(t * size, (t + 1) * size)
        gram = lax.dot_general(
            weighted[:, here], augmented[:, here], (((1,), (1,)), ((), ())),
            precision=HIGHEST, preferred_element_type=F32,
        )
        grams.append(pack(gram, members))
        pattern = jnp.int32(0)
        for g in range(blocks):
            pattern = pattern + jnp.where(tile_ref[t] == g, history[g], jnp.int32(0))
        patterns.append(pattern)
    for p in range(sums_ref.shape[0]):
        terms = [
            jnp.where(patterns[t] == p, F32(1.0), F32(0.0)) * grams[t] for t in range(tiles)
        ]
        sums_ref[p] = sum(terms[1:], terms[0])


def chain(sums_of, arranged, flag_ref, members, bands, blocks):
    lane = iota((members, LANES), 1)
    diagonal = lane == iota((members, LANES), 0)
    start = jnp.where(diagonal, F32(1.0), F32(0.0))
    maps = [start] * blocks
    tail_lane = iota((LANES - members, LANES), 1)
    tail_row = iota((LANES - members, LANES), 0)
    tail = jnp.where((tail_row == 0) & (tail_lane == members), F32(1.0), F32(0.0))
    steps = []

    def fold(sums, b):
        step, square = steps[b]
        new = []
        for r in range(len(sums) // 2):
            right = dot(sums[2 * r + 1], step)
            right = jnp.concatenate([right, jnp.zeros_like(tail)], axis=0)
            new.append(sums[2 * r] + dot(square, right))
        return new

    sums = sums_of(0)
    for b in range(bands):
        system = sums[0] + jnp.where(diagonal, F32(members - 1), F32(0.0))
        solved = invert(system, members)
        half = jnp.where(diagonal, F32(0.5), F32(0.0)) + (0.5 * (members - 1)) * solved
        top = jnp.where(lane == members, -solved, half)
        square = jnp.where(lane < members, top, F32(0.0))
        steps.append((jnp.concatenate([top, tail], axis=0), square))
        if b < bands - 1:
            sums = sums_of(b + 1)
            for k in range(b + 1):
                sums = fold(sums, k)
            arranged(b + 1)
        moved = dot(jnp.concatenate(maps, axis=0), steps[b][0])
        for g in range(blocks):
            here = moved[g * members : (g + 1) * members]
            maps[g] = jnp.where(flag_ref[b, g] > 0, here, maps[g])
    return maps


def solve_kernel(
    bands, cols, priors_hbm, innov_hbm, precision_hbm, tile_ref, count_ref, flag_ref,
    left_ref, swap_ref, priors_ref, innov_ref, precision_ref, sums_ref, parts_ref, final_ref,
    in_sems, send_swap, recv_swap, send_parts, recv_parts, send_band, recv_band, send_col, recv_col, send_relay,
):
    my_band, my_col = lax.axis_index("band"), lax.axis_index("col")
    owners = final_ref.shape[1] // ROWS
    members = priors_ref.shape[0]
    blocks = flag_ref.shape[1]
    loads = [
        pltpu.make_async_copy(src, dst, in_sems.at[i])
        for i, (src, dst) in enumerate(
            [(priors_hbm, priors_ref), (innov_hbm, innov_ref), (precision_hbm, precision_ref)]
        )
    ]
    for load in loads:
        load.start()
    core = lax.rem(my_col, 2)
    chip = my_col // 2
    partner = my_col + 1 - 2 * core
    chips = cols // 2
    wide, relayed = 2, 3
    barrier = pltpu.get_barrier_semaphore()

    def greet_col(d, carry):
        other = lax.rem(my_col + d, cols)
        pl.semaphore_signal(barrier, inc=1, device_id=(my_band, other), device_id_type=MESH)
        return carry

    def greet_band(d, carry):
        other = lax.rem(my_band + d, bands)
        pl.semaphore_signal(barrier, inc=1, device_id=(other, my_col), device_id_type=MESH)
        return carry

    lax.fori_loop(1, cols, greet_col, 0)
    lax.fori_loop(1, bands, greet_band, 0)
    for load in loads:
        load.wait()
    local_sums(priors_ref, innov_ref, precision_ref, tile_ref, count_ref, flag_ref, sums_ref, my_band)
    pl.semaphore_wait(barrier, cols + bands - 2)

    def rows_of(owner):
        return pl.ds(pl.multiple_of(owner * ROWS, ROWS), ROWS)

    def part_copy(band, source, owner, target):
        count = 2**band
        return pltpu.make_async_remote_copy(
            src_ref=sums_ref.at[pl.ds(0, count), rows_of(owner)],
            dst_ref=parts_ref.at[source, pl.ds(0, count)],
            send_sem=send_parts.at[owner],
            recv_sem=recv_parts.at[source],
            device_id=(my_band, target),
            device_id_type=MESH,
        )

    def band_copy(band, target):
        here = (pl.ds(2**band - 1, 2**band), rows_of(my_col))
        return pltpu.make_async_remote_copy(
            src_ref=final_ref.at[here],
            dst_ref=final_ref.at[here],
            send_sem=send_band.at[target],
            recv_sem=recv_band.at[band],
            device_id=(target, my_col),
            device_id_type=MESH,
        )

    def col_copy(band, owner, target):
        here = (pl.ds(2**band - 1, 2**band), rows_of(owner))
        return pltpu.make_async_remote_copy(
            src_ref=final_ref.at[here],
            dst_ref=final_ref.at[here],
            send_sem=send_col.at[band, target],
            recv_sem=recv_col.at[band, owner],
            device_id=(my_band, target),
            device_id_type=MESH,
        )

    def each_owner(action):
        def step(d, carry):
            owner = lax.rem(my_col + d, cols)

            @pl.when(owner < owners)
            def _():
                action(owner)

            return carry

        lax.fori_loop(1, cols, step, 0)

    def each_peer(action):
        def step(d, carry):
            action(lax.rem(my_col + d, cols))
            return carry

        lax.fori_loop(1, cols, step, 0)

    def col_targets(band, action):
        if band < relayed:
            each_peer(action)
        else:
            def step(d, carry):
                action(2 * lax.rem(chip + d, chips) + core)
                return carry

            lax.fori_loop(1, chips, step, 0)
            action(partner)

    def each_band(action):
        def step(d, carry):
            action(lax.rem(my_band + d, bands))
            return carry

        lax.fori_loop(1, bands, step, 0)

    def swap_copy(band, pair, side):
        count = 2**band
        return pltpu.make_async_remote_copy(
            src_ref=sums_ref.at[pl.ds(0, count), rows_of(2 * pair + side)],
            dst_ref=swap_ref.at[pair, pl.ds(0, count)],
            send_sem=send_swap.at[pair],
            recv_sem=recv_swap.at[pair],
            device_id=(my_band, partner),
            device_id_type=MESH,
        )

    def relay_copy(band, owner):
        here = (pl.ds(2**band - 1, 2**band), rows_of(owner))
        return pltpu.make_async_remote_copy(
            src_ref=final_ref.at[here],
            dst_ref=final_ref.at[here],
            send_sem=send_relay.at[band, owner],
            recv_sem=recv_col.at[band, owner],
            device_id=(my_band, partner),
            device_id_type=MESH,
        )

    def each_pair(action):
        def step(pair, carry):
            action(pair)
            return carry

        lax.fori_loop(0, owners // 2, step, 0)

    def each_alike(action):
        def step(d, carry):
            action(2 * lax.rem(chip + d, chips) + core)
            return carry

        lax.fori_loop(1, chips, step, 0)

    def owners_of(action):
        def step(owner):
            @pl.when(owner < owners)
            def _():
                action(owner)

        return step

    def part_targets(band, action):
        if band < wide:
            each_owner(action)
        else:
            each_alike(owners_of(action))

    for band in range(bands):

        @pl.when(my_band == band)
        def _(band=band):
            count = 2**band
            if band >= wide:
                each_pair(lambda pair: swap_copy(band, pair, 1 - core).start())

                def join(pair):
                    swap_copy(band, pair, core).wait_recv()
                    rows = rows_of(2 * pair + core)
                    sums_ref[:count, rows] = sums_ref[:count, rows] + swap_ref[pair, :count]

                each_pair(join)
            part_targets(band, lambda owner: part_copy(band, my_col, owner, owner).start())

    for band in range(bands):

        @pl.when((my_band == band) & (my_col < owners))
        def _(band=band):
            count = 2**band

            def add(source, total):
                part_copy(band, source, my_col, source).wait_recv()
                return total + parts_ref[source, :count]

            start = sums_ref[:count, rows_of(my_col)]
            if band < wide:
                total = lax.fori_loop(
                    1, cols, lambda d, t: add(lax.rem(my_col + d, cols), t), start
                )
            else:
                total = lax.fori_loop(
                    1, chips, lambda d, t: add(2 * lax.rem(chip + d, chips) + core, t), start
                )
            final_ref[count - 1 : 2 * count - 1, rows_of(my_col)] = total
            each_band(lambda target: band_copy(band, target).start())
            col_targets(band, lambda target: col_copy(band, my_col, target).start())

    def forward(band):
        @pl.when((my_band != band) & (my_col < owners))
        def _():
            band_copy(band, lax.rem(my_band + 1, bands)).wait_recv()
            col_targets(band, lambda target: col_copy(band, my_col, target).start())

    def relay(band):
        def pass_on(owner):
            col_copy(band, owner, owner).wait_recv()
            relay_copy(band, owner).start()

        each_alike(owners_of(pass_on))

    forward(0)
    def sums_of(band):
        if band == 0:
            for b in range(1, min(bands, relayed)):
                forward(b)
        elif band == 1:
            for b in range(relayed, bands):
                forward(b)
        if band < relayed:
            each_owner(lambda owner: col_copy(band, owner, owner).wait_recv())
        else:
            each_pair(lambda pair: relay_copy(band, 2 * pair + 1 - core).wait_recv())
        first = 2**band - 1
        return [unpack(final_ref[first + p], members) for p in range(2**band)]

    def arranged(band):
        if band + 1 >= relayed and band + 1 < bands:
            relay(band + 1)

    maps = chain(sums_of, arranged, flag_ref, members, bands, blocks)
    for g in range(blocks):
        high = maps[g].astype(BF16).astype(F32)
        low = maps[g] - high
        pad = jnp.zeros((2 * LANES - 3 * members, LANES), F32)
        stacked = jnp.concatenate([high, low, high, pad], axis=0)
        left = jnp.concatenate([stacked[:LANES].T, stacked[LANES:].T], axis=1)
        left_ref[g] = left[: left_ref.shape[1]].astype(BF16)

    for band in range(bands):

        @pl.when(my_band == band)
        def _(band=band):
            if band >= wide:
                each_pair(lambda pair: swap_copy(band, pair, 1 - core).wait_send())
            part_targets(band, lambda owner: part_copy(band, my_col, owner, owner).wait_send())

            @pl.when(my_col < owners)
            def _():
                each_band(lambda target: band_copy(band, target).wait_send())

        @pl.when(my_col < owners)
        def _(band=band):
            col_targets(band, lambda target: col_copy(band, my_col, target).wait_send())

        if band >= relayed:
            each_alike(owners_of(lambda owner: relay_copy(band, owner).wait_send()))


def apply_kernel(
    left_ref, mean_hbm, state_hbm, mean_out, out_hbm,
    state_ref, out_ref, mean_ref, moved_ref, in_sems, out_sems, mean_sems,
):
    blocks, levels, members, columns = state_hbm.shape
    pieces = in_sems.shape[0] // blocks
    size = levels // pieces

    def place(i):
        return i // pieces, pl.ds(lax.rem(i, pieces) * size, size)

    def load(i):
        here = place(i)
        return pltpu.make_async_copy(state_hbm.at[here], state_ref.at[here], in_sems.at[i])

    def store(i):
        here = place(i)
        return pltpu.make_async_copy(out_ref.at[here], out_hbm.at[here], out_sems.at[i])

    def each(action):
        def step(i, carry):
            action(i)
            return carry

        lax.fori_loop(0, blocks * pieces, step, 0)

    mean_load = pltpu.make_async_copy(mean_hbm, mean_ref, mean_sems.at[0])
    mean_load.start()
    each(lambda i: load(i).start())
    mean_load.wait()

    def work(i):
        load(i).wait()
        g = i // pieces
        left = left_ref[g][:, : 3 * members]
        for k in range(size):
            l = lax.rem(i, pieces) * size + k
            value = state_ref[g, l]
            high = value.astype(BF16)
            low = (value - high.astype(F32)).astype(BF16)
            right = jnp.concatenate([high, high, low], axis=0)
            result = jnp.dot(left, right, preferred_element_type=F32)
            out_ref[g, l] = result[:members]
            here = (g, pl.ds(l, 1))
            moved_ref[here] = mean_ref[here] - result[members : members + 1]
        store(i).start()

    each(work)
    mean_store = pltpu.make_async_copy(moved_ref, mean_out, mean_sems.at[1])
    mean_store.start()
    each(lambda i: store(i).wait())
    mean_store.wait()


def local(
    obs_priors,
    innovation,
    obs_precision,
    tile_block,
    obs_count,
    block_mask,
    prior_state_mean,
    prior_state_deviation,
):
    members, rows = obs_priors.shape
    blocks, levels, _, columns = prior_state_deviation.shape
    bands, cols = lax.axis_size("band"), lax.axis_size("col")
    kept, _ = packed_rows(members)
    owners = kept // ROWS
    smem = pl.BlockSpec(memory_space=pltpu.SMEM)
    vmem = pl.BlockSpec(memory_space=pltpu.VMEM)
    hbm = pl.BlockSpec(memory_space=pl.ANY)
    dma = pltpu.SemaphoreType.DMA
    left = pl.pallas_call(
        functools.partial(solve_kernel, bands, cols),
        out_shape=jax.ShapeDtypeStruct((blocks, members + 2 * ROWS, 2 * LANES), BF16),
        in_specs=[hbm, hbm, hbm, smem, smem, smem],
        out_specs=vmem,
        scratch_shapes=[
            pltpu.VMEM((owners // 2, 2 ** (bands - 1), ROWS, LANES), F32),
            pltpu.VMEM((members, rows), F32),
            pltpu.VMEM((1, rows), F32),
            pltpu.VMEM((1, rows), F32),
            pltpu.VMEM((2 ** (bands - 1), kept, LANES), F32),
            pltpu.VMEM((cols, 2 ** (bands - 1), ROWS, LANES), F32),
            pltpu.VMEM((2**bands - 1, kept, LANES), F32),
            dma((3,)),
            dma((owners // 2,)),
            dma((owners // 2,)),
            dma((owners,)),
            dma((cols,)),
            dma((bands,)),
            dma((bands,)),
            dma((bands, cols)),
            dma((bands, owners)),
            dma((bands, owners)),
        ],
        compiler_params=pltpu.CompilerParams(
            collective_id=0, has_side_effects=True, vmem_limit_bytes=56 * 1024 * 1024
        ),
    )(obs_priors, innovation[None], obs_precision[None], tile_block, obs_count, block_mask)
    pieces = 4
    return pl.pallas_call(
        apply_kernel,
        out_shape=(
            jax.ShapeDtypeStruct(prior_state_mean.shape, F32),
            jax.ShapeDtypeStruct(prior_state_deviation.shape, F32),
        ),
        in_specs=[vmem, hbm, hbm],
        out_specs=(hbm, hbm),
        scratch_shapes=[
            pltpu.VMEM(prior_state_deviation.shape, F32),
            pltpu.VMEM(prior_state_deviation.shape, F32),
            pltpu.VMEM(prior_state_mean.shape, F32),
            pltpu.VMEM(prior_state_mean.shape, F32),
            dma((blocks * pieces,)),
            dma((blocks * pieces,)),
            dma((2,)),
        ],
        compiler_params=pltpu.CompilerParams(vmem_limit_bytes=56 * 1024 * 1024),
    )(left, prior_state_mean, prior_state_deviation)


def solution(mesh):
    placed = (
        P(None, ("band", "col")),
        P(("band", "col")),
        P(("band", "col")),
        P(("band", "col")),
        P(("band", "col")),
        P(None, "col"),
        P("col", None, "band"),
        P("col", None, None, "band"),
    )
    return jax.shard_map(
        local,
        mesh=mesh,
        in_specs=placed,
        out_specs=(P("col", None, "band"), P("col", None, None, "band")),
        check_vma=False,
    )
```
